256 devices in a mesh: ctx: 32 (over z, x), head: 8 (over y, core).
Axes of the slice: x: 4, y: 4, z: 8, core: 2. Of those that a mesh axis runs over, the one named last changes fastest.
Arguments:
- queries: bfloat16 [2048, 16, 128], P('ctx', 'head'), may hold values from -9 to 9
- cache_keys: bfloat16 [65536, 128], P('ctx'), may hold values from -15 to 15
- cache_values: bfloat16 [65536, 128], P('ctx'), may hold values from -6 to 6
- page_table: int32 [32, 4], P('ctx'), may hold values from 0 to 3, each once within a row
- page_count: int32 [32], P('ctx'), may hold values from 1 to 4, as said below
- new_kv: bfloat16 [2048, 2, 128], P(('ctx', 'head')), may hold values from -15 to 15
- new_owner: int32 [2048], replicated, may hold values from 0 to 31, as said below
- new_offset: int32 [2048], replicated, may hold values from 0 to 127
Outputs:
- attended: bfloat16 [2048, 16, 128], P('ctx', 'head')
- appended: bfloat16 [4096, 2, 128], P('ctx')
The draws below stay inside these ranges and needn't reach their ends.
Inputs may be any that keep to these rules, and one draw needn't show every extreme that they name: `page_count`: some store has all 4 pages live. `page_table`: each row names every page once. `new_owner`: no two new tokens share a pair of owner and offset; some store's 128 rows are all taken.
All inputs are finite; a program needn't handle non-finite values.
Results may differ from the reference program's by a relative error of at most 0.0028.
Values may be sent and summed in bfloat16 or wider, within the bound.
No kernel may reach another device: no remote copies, remote signals or barrier semaphores. Data moves between devices by JAX's collectives and lax.ppermute only.
A program may use at most 64 MiB of HBM per device.

```python
import math
import jax
import jax.numpy as jnp
from jax import lax

HEADS = 16
HD = 128
PAGE = 512
SLOTS = 4
NEW = 2048
APPEND = 128
CACHE_ROWS = 65536
N_CTX = 32


def owner_slots(key):
    total = N_CTX * APPEND
    first, second, third = jax.random.split(jax.random.fold_in(key, 104), 3)
    fullest = jax.random.randint(first, (), 0, N_CTX)
    ranks = jax.random.permutation(second, total)
    owners = jnp.arange(total) // APPEND
    ranks = jnp.where(owners == fullest, ranks - total, ranks)
    order = jnp.argsort(ranks, stable=True)
    chosen = jax.random.permutation(third, order[:NEW])
    return chosen.astype(jnp.int32)


def draw_queries(key, part):
    key = jax.random.fold_in(key, 1)
    result = 1.5 * jax.random.truncated_normal(key, -6.0, 6.0, (NEW, HEADS, HD))
    return result.astype(jnp.bfloat16)


def draw_new_kv(key, part):
    key = jax.random.fold_in(key, 2)
    first, second = jax.random.split(key)
    key_rows = 2.5 * jax.random.truncated_normal(first, -6.0, 6.0, (NEW, HD))
    value_rows = jax.random.truncated_normal(second, -6.0, 6.0, (NEW, HD))
    return jnp.stack([key_rows, value_rows], axis=1).astype(jnp.bfloat16)


def draw_page_count(key, part):
    key = jax.random.fold_in(key, 3)
    first, second = jax.random.split(key)
    counts = jax.random.randint(first, (N_CTX,), 1, SLOTS // 2 + 1)
    fullest = jax.random.randint(second, (), 0, N_CTX)
    return counts.at[fullest].set(SLOTS).astype(jnp.int32)


def draw_new_owner(key, part):
    chosen = owner_slots(key)
    return (chosen // APPEND).astype(jnp.int32)


def draw_new_offset(key, part):
    chosen = owner_slots(key)
    return (chosen % APPEND).astype(jnp.int32)


def block_levels(stream_key, shape, cuts, smallest, high):
    level, own = 1.0, jax.random.fold_in(stream_key, 6)
    for axis_at, shards_of in cuts:
        steps = jnp.exp(jax.random.uniform(jax.random.fold_in(own, axis_at), (shards_of,), jnp.float32, smallest / len(cuts), high / len(cuts)))
        level = level * jnp.repeat(steps, shape[axis_at] // shards_of).reshape([-1 if axis == axis_at else 1 for axis in range(len(shape))])
    return level


def normal_values(rng, extent, scale, limit, cuts=(), held_as=jnp.bfloat16):
    values = scale * jax.random.normal(rng, extent, jnp.float32)
    if cuts:
        values = values * block_levels(rng, extent, cuts, -0.22, 0.18)
    return jnp.clip(values, -limit, limit).astype(held_as)


def setup_inputs(seed: int = 0) -> dict:
    splits = jax.random.split(jax.random.key(seed), 9)
    queries = draw_queries(jax.random.fold_in(splits[8], 71), 0)
    cache_keys = normal_values(splits[1], (CACHE_ROWS, HD), 2.5, 15.0, ((0, 32),))
    cache_values = normal_values(splits[2], (CACHE_ROWS, HD), 1.0, 6.0, ((0, 32),))
    page_table = jax.vmap(lambda own: jax.random.permutation(own, SLOTS))(jax.random.split(splits[3], N_CTX)).reshape((N_CTX, SLOTS)).astype(jnp.int32)
    page_count = draw_page_count(jax.random.fold_in(splits[8], 71), 0)
    new_kv = draw_new_kv(jax.random.fold_in(splits[8], 71), 0)
    new_owner = draw_new_owner(jax.random.fold_in(splits[8], 71), 0)
    new_offset = draw_new_offset(jax.random.fold_in(splits[8], 71), 0)
    return dict(queries=queries, cache_keys=cache_keys, cache_values=cache_values, page_table=page_table, page_count=page_count, new_kv=new_kv, new_owner=new_owner, new_offset=new_offset)


def block_partial(scores, values):
    maxima = lax.optimization_barrier(jnp.max(scores, axis=1))
    weights = jnp.exp(scores - maxima[:, None])
    totals = lax.optimization_barrier(jnp.sum(weights, axis=1))
    summed = jnp.dot(weights.astype(jnp.bfloat16), values, preferred_element_type=jnp.float32)
    return (maxima, totals, summed)

def join_partials(first, second):
    combined = jnp.maximum(first[0], second[0])
    factor_one = jnp.exp(first[0] - combined)
    factor_two = jnp.exp(second[0] - combined)
    totals = first[1] * factor_one + second[1] * factor_two
    summed = first[2] * factor_one[:, None] + second[2] * factor_two[:, None]
    return (combined, totals, summed)

def reference(queries, cache_keys, cache_values, page_table, page_count, new_kv, new_owner, new_offset):
    scaling = 1.0 / math.sqrt(HD)
    query_rows = queries.reshape(NEW * HEADS, HD)
    count_rows = NEW * HEADS
    page_slots = jnp.arange(SLOTS, dtype=jnp.int32)

    def one_store(carry, item):
        store_keys, store_values, table_row, live_count = item
        taken = page_slots < live_count
        page_live = jnp.any((table_row[:, None] == page_slots[None, :]) & taken[:, None], axis=0)
        row_live = jnp.repeat(page_live, PAGE)
        scores = lax.dot_general(query_rows, store_keys, (((1,), (1,)), ((), ())), preferred_element_type=jnp.float32) * scaling
        scores = jnp.where(row_live[None, :], scores, jnp.float32(-1e+30))
        found = block_partial(scores, store_values)
        return (join_partials(carry, found), None)
    initial = (jnp.full((count_rows,), -1e+30, jnp.float32), jnp.zeros((count_rows,), jnp.float32), jnp.zeros((count_rows, HD), jnp.float32))
    stacked = (cache_keys.reshape(N_CTX, SLOTS * PAGE, HD), cache_values.reshape(N_CTX, SLOTS * PAGE, HD), page_table, page_count)
    cache_part, unused = lax.scan(one_store, initial, stacked)
    scores = lax.dot_general(query_rows, new_kv[:, 0], (((1,), (1,)), ((), ())), preferred_element_type=jnp.float32) * scaling
    positions = jnp.arange(count_rows, dtype=jnp.int32) // HEADS
    visible = jnp.arange(NEW, dtype=jnp.int32)[None, :] <= positions[:, None]
    scores = jnp.where(visible, scores, jnp.float32(-1e+30))
    self_part = block_partial(scores, new_kv[:, 1])
    maxima, totals, summed = join_partials(cache_part, self_part)
    attended = (summed / totals[:, None]).reshape(NEW, HEADS, HD).astype(jnp.bfloat16)
    target = (new_owner * APPEND + new_offset).astype(jnp.int32)
    appended = jnp.zeros((N_CTX * APPEND, 2, HD), jnp.bfloat16).at[target].set(new_kv)
    return (attended, appended)
```

```python
import functools
import math

import jax
import jax.numpy as jnp
from jax import lax
from jax.experimental import pallas as pl
from jax.experimental.pallas import tpu as pltpu
from jax.sharding import Mesh, PartitionSpec as P

F32 = jnp.float32
BF16 = jnp.bfloat16
I32 = jnp.int32
HD = 128
PAGES = 4
HALF = 256
KEYS = 2 * HALF
SIDE = PAGES * HALF
QROWS = 1024
TILE = 256
BLOCK = 128
NEG = -1e30
SCALE = 1.4426950408889634 / math.sqrt(HD)
FIXED = float(1 << 18)
PAYLOAD = 144
SENT = 160


def shifted(value, axis, steps):
    count = lax.axis_size(axis)
    return lax.ppermute(value, axis, [(i, (i + steps) % count) for i in range(count)])


def swapped(value, axis, bit):
    count = lax.axis_size(axis)
    return lax.ppermute(value, axis, [(i, i ^ bit) for i in range(count)])


def across(row):
    return jnp.transpose(jnp.broadcast_to(row, (BLOCK, BLOCK)), (1, 0))


def split_fixed(value):
    fixed = jnp.round(value * FIXED).astype(I32)
    return [fixed >> 16, (fixed & 0xFFFF) - 32768]


def join_fixed(high, low):
    return (high * 65536 + (low + 32768)).astype(F32) * (1.0 / FIXED)


def page_parts(ref, p, start=0, stride=HALF):
    return ref[pl.ds(pl.multiple_of(start + p * stride, HALF), HALF), :]


def score_pages(q, scores, top, slot, mask, keys_at):
    def page(p, carry):
        @pl.when(((mask >> p) & 1) != 0)
        def _():
            for i, keys in enumerate(keys_at(p)):
                for t in range(QROWS // TILE):
                    rows = pl.ds(t * TILE, TILE)
                    s = lax.dot_general(
                        q[rows, :], keys, (((1,), (1,)), ((), ())), preferred_element_type=F32
                    )
                    scores[slot + p, rows, i * HALF : (i + 1) * HALF] = s
                    top[rows, :] = jnp.maximum(
                        top[rows, :], jnp.maximum(s[:, :HD], s[:, HD:])
                    )

        return carry

    lax.fori_loop(0, PAGES, page, 0)


def weigh(scores_at, values, level, total, acc, width):
    for t in range(QROWS // TILE):
        rows = pl.ds(t * TILE, TILE)
        now = level[rows, :]
        s = scores_at(rows)
        parts = [
            jnp.exp2((s[:, j * HD : (j + 1) * HD] - now) * SCALE) for j in range(width // HD)
        ]
        total[rows, :] = total[rows, :] + functools.reduce(jnp.add, parts)
        weight = jnp.concatenate([e.astype(BF16) for e in parts], axis=1)
        acc[rows, :] = acc[rows, :] + jnp.dot(weight, values, preferred_element_type=F32)


def weigh_pages(scores, level, total, acc, slot, mask, values_at):
    def page(p, carry):
        @pl.when(((mask >> p) & 1) != 0)
        def _():
            values = jnp.concatenate(values_at(p), axis=0)
            weigh(lambda rows: scores[slot + p, rows, :], values, level, total, acc, KEYS)

        return carry

    lax.fori_loop(0, PAGES, page, 0)


def settle(top, level):
    found = []
    for b in range(QROWS // BLOCK):
        rows = pl.ds(b * BLOCK, BLOCK)
        row = jnp.max(jnp.transpose(top[rows, :], (1, 0)), axis=0, keepdims=True)
        level[rows, :] = across(row)
        found.append(row)
    return found


def mask_of(ref, start=2 * SIDE):
    return jnp.sum(ref[start : start + 16, :].astype(F32)).astype(I32)


def here():
    return [lax.axis_index(a) for a in ("z", "x", "y", "core")]


def load_queries(q, q3):
    for b in range(8):
        q[pl.ds(b * BLOCK, BLOCK), :] = q3[b, 0:BLOCK, :]


def gather_kernel(queries, near, far, out):
    for b in range(8):
        out[b, 0:BLOCK, :] = queries[...]
        out[b, BLOCK : BLOCK + 16, :] = near[...]
        out[b, BLOCK + 16 : SENT, :] = far[...]


def first_kernel(
    table, live, q3, ok, ov, an, af, bn, bf, level, total, acc, q, scores, top
):
    load_queries(q, q3)
    top[...] = jnp.full(top.shape, NEG, F32)
    total[...] = jnp.zeros(total.shape, F32)
    acc[...] = jnp.zeros(acc.shape, F32)
    own = 0
    for k in range(PAGES):
        own = own + jnp.where(k < live[0], jnp.left_shift(1, table[0, k]), 0)
    stores = [
        (
            own,
            lambda p: [page_parts(ok, p, 0, KEYS), page_parts(ok, p, HALF, KEYS)],
            lambda p: [page_parts(ov, p, 0, KEYS), page_parts(ov, p, HALF, KEYS)],
        )
    ]
    for near, far in ((an, af), (bn, bf)):
        stores.append(
            (
                mask_of(near),
                lambda p, near=near, far=far: [page_parts(near, p), page_parts(far, p)],
                lambda p, near=near, far=far: [page_parts(near, p, SIDE), page_parts(far, p, SIDE)],
            )
        )
    for i, (mask, keys_at, _) in enumerate(stores):
        score_pages(q, scores, top, i * PAGES, mask, keys_at)
    settle(top, level)
    for i, (mask, _, values_at) in enumerate(stores):
        weigh_pages(scores, level, total, acc, i * PAGES, mask, values_at)


def second_kernel(
    q3, ckn, cvn, ckf, cvf, new, level_in, total_in, acc_in, out,
    q, scores, fresh, top, level, total, acc,
):
    z, x, y, core = here()
    load_queries(q, q3)
    top[...] = level_in[...]
    mask = mask_of(cvn, SIDE)
    score_pages(q, scores, top, 0, mask, lambda p: [page_parts(ckn, p), page_parts(ckf, p)])

    at = lax.broadcasted_iota(I32, (BLOCK, BLOCK), 0)
    place = lax.broadcasted_iota(I32, (BLOCK, BLOCK), 1) == (at % 64) * 2 + at // 64
    place = jnp.where(place, 1.0, 0.0).astype(BF16)
    apart = [
        jnp.dot(place, new[g * BLOCK : (g + 1) * BLOCK, :], preferred_element_type=F32).astype(BF16)
        for g in range(4)
    ]
    keys = jnp.concatenate([n[0:64, :] for n in apart], axis=0)
    values = jnp.concatenate([n[64:BLOCK, :] for n in apart], axis=0)
    slot = lax.broadcasted_iota(I32, (TILE, 256), 1)
    side = jnp.where(slot < 128, jnp.where(z < 4, 0, 3), jnp.where(z < 4, 2, 1))
    head = ((y + side) & 3) * 2 + (core ^ ((slot // 8) & 1))
    token = ((slot // 16) % 8 * 4 + ((x + z) & 3)) * 64 + head * 8 + slot % 8
    row = lax.broadcasted_iota(I32, (TILE, 256), 0)
    for t in range(QROWS // TILE):
        rows = pl.ds(t * TILE, TILE)
        s = lax.dot_general(q[rows, :], keys, (((1,), (1,)), ((), ())), preferred_element_type=F32)
        position = ((2 * t + row // BLOCK) * 4 + x) * 64 + (row % BLOCK) // 2
        s = jnp.where(token <= position, s, NEG)
        fresh[rows, :] = s
        top[rows, :] = jnp.maximum(top[rows, :], jnp.maximum(s[:, :HD], s[:, HD:]))
    peaks = settle(top, level)
    for t in range(QROWS // TILE):
        rows = pl.ds(t * TILE, TILE)
        factor = jnp.exp2((level_in[rows, :] - level[rows, :]) * SCALE)
        total[rows, :] = total_in[rows, :] * factor
        acc[rows, :] = acc_in[rows, :] * factor
    weigh_pages(
        scores, level, total, acc, 0, mask, lambda p: [page_parts(cvn, p), page_parts(cvf, p)]
    )
    weigh(lambda rows: fresh[rows, :], values, level, total, acc, 256)

    for j in range(8):
        rows = pl.ds(j * BLOCK, BLOCK)
        full = acc[rows, :]
        size = jnp.max(jnp.transpose(jnp.abs(full), (1, 0)), axis=0, keepdims=True)
        size = jnp.maximum(size, 1e-30)
        number = jnp.round(full * across(32767.0 / size)).astype(I32).astype(jnp.int16)
        weight = jnp.sum(jnp.transpose(total[rows, :], (1, 0)), axis=0, keepdims=True)
        stats = (
            split_fixed(peaks[j] * SCALE)
            + split_fixed(jnp.log2(weight))
            + split_fixed(jnp.log2(size))
        )
        stats = jnp.concatenate(stats + [jnp.zeros((10, BLOCK), I32)], axis=0)
        out[j] = jnp.concatenate([number, stats.astype(jnp.int16)], axis=0)


def merge_kernel(parts, out):
    stats = [parts[s, BLOCK:PAYLOAD, :].astype(I32) for s in range(8)]

    def rows(at):
        return jnp.concatenate(
            [join_fixed(s[at : at + 1, :], s[at + 1 : at + 2, :]) for s in stats], axis=0
        )

    peak, weight, size = rows(0), rows(2), rows(4)
    peak = peak - jnp.max(peak, axis=0, keepdims=True)
    whole = jnp.sum(jnp.exp2(peak + weight), axis=0, keepdims=True)
    factor = jnp.exp2(peak + size) / (whole * 32767.0)
    columns = jnp.transpose(factor, (1, 0))
    total = jnp.zeros((BLOCK, HD), F32)
    for s in range(8):
        total = total + parts[s, 0:BLOCK, :].astype(F32) * columns[:, s : s + 1]
    out[...] = total.astype(BF16)


def route_kernel(r0, r1, r2, r3, code, o0, o1, o2, o3):
    z, x, y, core = here()
    target = lax.broadcasted_iota(I32, (4 * 256, 256), 0)
    lane = lax.broadcasted_iota(I32, (4 * 256, 256), 1)
    store = z * 4 + ((x + target // 256) & 3)
    want = jnp.where((target & 1) == (lane & 1), store * 128 + (target % 256) // 2, -1)
    total = jnp.zeros((4 * 256, HD), F32)
    for j, r in enumerate((r0, r1, r2, r3)):
        have = code[pl.ds((y + (0, 3, 1, 2)[j]) & 3, 1), :]
        chosen = jnp.where(want == have, 1.0, 0.0).astype(BF16)
        total = total + jnp.dot(chosen, r[...], preferred_element_type=F32)
    total = total.astype(BF16)
    for d, o in enumerate((o0, o1, o2, o3)):
        o[...] = total[d * 256 : (d + 1) * 256, :]


def place_kernel(n0, n1, n2, n3, out):
    total = n0[...].astype(F32) + n1[...].astype(F32)
    total = total + n2[...].astype(F32) + n3[...].astype(F32)
    out[...] = total.astype(BF16)


def after(value, *others):
    def kernel(*refs):
        pass

    return pl.pallas_call(
        kernel,
        out_shape=jax.ShapeDtypeStruct(value.shape, value.dtype),
        in_specs=[pl.BlockSpec(memory_space=pl.ANY)] * (1 + len(others)),
        out_specs=pl.BlockSpec(memory_space=pl.ANY),
        input_output_aliases={0: 0},
        name="after",
    )(value, *others)


def smem():
    return pl.BlockSpec(memory_space=pltpu.SMEM)


def vmem():
    return pl.BlockSpec(memory_space=pltpu.VMEM)


def cost(pages):
    return pl.CostEstimate(
        flops=4 * QROWS * KEYS * HD * pages,
        bytes_accessed=1 << 20,
        transcendentals=QROWS * KEYS * pages,
    )


def shards(
    queries, cache_keys, cache_values, page_table, page_count, new_kv, new_owner, new_offset
):
    z, x = lax.axis_index("z"), lax.axis_index("x")
    y, core = lax.axis_index("y"), lax.axis_index("core")

    bits = jnp.where(jnp.arange(PAGES) < page_count[0], 1 << page_table[0], 0)
    bits_row = jnp.pad(bits.astype(BF16)[None, :], ((0, 15), (0, HD - PAGES)))
    halves = [
        lax.dynamic_index_in_dim(a.reshape(PAGES, 2, HALF, HD), core, 1, keepdims=False).reshape(
            SIDE, HD
        )
        for a in (cache_keys, cache_values)
    ]
    halves = jnp.concatenate(halves + [bits_row], axis=0)
    an, bn = shifted(halves, "x", 1), shifted(halves, "x", -1)
    ckn, cvn = shifted(an[:SIDE], "x", 1), shifted(bn[SIDE:], "x", -1)
    af, bf, ckf, cvf = [swapped(a, "core", 1) for a in (an, bn, ckn, cvn)]

    near = new_kv.reshape(16, HD)
    far = swapped(near, "core", 1)
    sent = pl.pallas_call(
        gather_kernel,
        out_shape=jax.ShapeDtypeStruct((8, SENT, HD), BF16),
        in_specs=[vmem()] * 3,
        out_specs=vmem(),
        name="gather",
    )(queries.reshape(BLOCK, HD), near, far)
    q3 = lax.all_to_all(sent, "z", 0, 0)
    rows = q3[:, BLOCK:, :].reshape(256, HD)
    rows = [rows, shifted(rows, "y", 1), shifted(rows, "y", -1), shifted(rows, "y", 2)]
    lower = z < 4
    new = jnp.concatenate(
        [jnp.where(lower, rows[0], rows[1]), jnp.where(lower, rows[3], rows[2])], axis=0
    )
    new = lax.ppermute(
        new, ("z", "x"), [(p * 4 + (i + p) % 4, p * 4 + i) for p in range(8) for i in range(4)]
    )

    state = jax.ShapeDtypeStruct((QROWS, HD), F32)
    params = pltpu.CompilerParams(vmem_limit_bytes=48 * 1024 * 1024)
    level, total, acc = pl.pallas_call(
        first_kernel,
        out_shape=(state,) * 3,
        in_specs=[smem()] * 2 + [vmem()] * 7,
        out_specs=(vmem(),) * 3,
        scratch_shapes=[
            pltpu.VMEM((QROWS, HD), BF16),
            pltpu.VMEM((3 * PAGES, QROWS, KEYS), F32),
            pltpu.VMEM((QROWS, HD), F32),
        ],
        compiler_params=params,
        cost_estimate=cost(6),
        name="first",
    )(page_table, page_count, q3, cache_keys, cache_values, an, af, bn, bf)
    payload = pl.pallas_call(
        second_kernel,
        out_shape=jax.ShapeDtypeStruct((8, PAYLOAD, HD), jnp.int16),
        in_specs=[vmem()] * 9,
        out_specs=vmem(),
        scratch_shapes=[
            pltpu.VMEM((QROWS, HD), BF16),
            pltpu.VMEM((PAGES, QROWS, KEYS), F32),
            pltpu.VMEM((QROWS, 256), F32),
        ]
        + [pltpu.VMEM((QROWS, HD), F32)] * 4,
        compiler_params=params,
        cost_estimate=cost(2),
        name="second",
    )(q3, ckn, cvn, ckf, cvf, new, level, total, acc)

    code = (new_owner * 128 + new_offset).reshape(8, 4, 4, 2, 8)
    code = lax.dynamic_index_in_dim(code, x, 1, keepdims=False)
    code = jnp.where(core == 1, jnp.flip(code, 2), code)
    code = jnp.repeat(jnp.transpose(code, (1, 0, 2, 3)).reshape(4, 128), 2, axis=1)
    code = after(code, payload)
    piece = jax.ShapeDtypeStruct((256, HD), BF16)
    t0, to_after, to_opposite, to_before = pl.pallas_call(
        route_kernel,
        out_shape=(piece,) * 4,
        in_specs=[vmem()] * 5,
        out_specs=(vmem(),) * 4,
        name="route",
    )(*rows, code)
    t1 = shifted(to_after, "x", 1)
    t2 = shifted(to_before, "x", -1)
    t3 = shifted(to_opposite, "x", 2)
    parts = lax.all_to_all(payload, "z", 0, 0)
    attended = pl.pallas_call(
        merge_kernel,
        out_shape=jax.ShapeDtypeStruct((BLOCK, HD), BF16),
        in_specs=[vmem()],
        out_specs=vmem(),
        name="merge",
    )(parts)
    appended = pl.pallas_call(
        place_kernel,
        out_shape=jax.ShapeDtypeStruct((256, HD), BF16),
        in_specs=[vmem()] * 4,
        out_specs=vmem(),
        name="place",
    )(t0, t1, t2, t3)
    return attended.reshape(queries.shape), appended.reshape(BLOCK, 2, HD)


def solution(mesh):
    grid = Mesh(mesh.devices.reshape(8, 4, 4, 2), ("z", "x", "y", "core"))
    ctx, head = ("z", "x"), ("y", "core")
    in_specs = (
        P(ctx, head, None),
        P(ctx, None),
        P(ctx, None),
        P(ctx, None),
        P(ctx),
        P(ctx + head, None, None),
        P(),
        P(),
    )
    out_specs = (P(ctx, head, None), P(ctx, None, None))
    return jax.shard_map(shards, mesh=grid, in_specs=in_specs, out_specs=out_specs, check_vma=False)
```

```python
import functools
import math

import jax
import jax.numpy as jnp
from jax import lax
from jax.experimental import pallas as pl
from jax.experimental.pallas import tpu as pltpu
from jax.sharding import Mesh, PartitionSpec as P

F32 = jnp.float32
BF16 = jnp.bfloat16
I32 = jnp.int32
HD = 128
PAGES = 4
HALF = 256
KEYS = 2 * HALF
SIDE = PAGES * HALF
QROWS = 1024
TILE = 256
BLOCK = 128
NEG = -1e30
SCALE = 1.4426950408889634 / math.sqrt(HD)
FIXED = float(1 << 18)
PAYLOAD = 144
SENT = 160


def shifted(value, axis, steps):
    count = lax.axis_size(axis)
    return lax.ppermute(value, axis, [(i, (i + steps) % count) for i in range(count)])


def swapped(value, axis, bit):
    count = lax.axis_size(axis)
    return lax.ppermute(value, axis, [(i, i ^ bit) for i in range(count)])


def across(row):
    return jnp.transpose(jnp.broadcast_to(row, (BLOCK, BLOCK)), (1, 0))


def split_fixed(value):
    fixed = jnp.round(value * FIXED).astype(I32)
    return [fixed >> 16, (fixed & 0xFFFF) - 32768]


def join_fixed(high, low):
    return (high * 65536 + (low + 32768)).astype(F32) * (1.0 / FIXED)


def page_parts(ref, p, start=0, stride=HALF):
    return ref[pl.ds(pl.multiple_of(start + p * stride, HALF), HALF), :]


def score_pages(q, scores, top, slot, mask, keys_at):
    def page(p, carry):
        @pl.when(((mask >> p) & 1) != 0)
        def _():
            for i, keys in enumerate(keys_at(p)):
                for t in range(QROWS // TILE):
                    rows = pl.ds(t * TILE, TILE)
                    s = lax.dot_general(
                        q[rows, :], keys, (((1,), (1,)), ((), ())), preferred_element_type=F32
                    )
                    scores[slot + p, rows, i * HALF : (i + 1) * HALF] = s
                    top[rows, :] = jnp.maximum(
                        top[rows, :], jnp.maximum(s[:, :HD], s[:, HD:])
                    )

        return carry

    lax.fori_loop(0, PAGES, page, 0)


def weigh(scores_at, values, level, total, acc, width):
    for t in range(QROWS // TILE):
        rows = pl.ds(t * TILE, TILE)
        now = level[rows, :]
        s = scores_at(rows)
        parts = [
            jnp.exp2((s[:, j * HD : (j + 1) * HD] - now) * SCALE) for j in range(width // HD)
        ]
        total[rows, :] = total[rows, :] + functools.reduce(jnp.add, parts)
        weight = jnp.concatenate([e.astype(BF16) for e in parts], axis=1)
        acc[rows, :] = acc[rows, :] + jnp.dot(weight, values, preferred_element_type=F32)


def weigh_pages(scores, level, total, acc, slot, mask, values_at):
    def page(p, carry):
        @pl.when(((mask >> p) & 1) != 0)
        def _():
            values = jnp.concatenate(values_at(p), axis=0)
            weigh(lambda rows: scores[slot + p, rows, :], values, level, total, acc, KEYS)

        return carry

    lax.fori_loop(0, PAGES, page, 0)


def settle(top, level):
    found = []
    for b in range(QROWS // BLOCK):
        rows = pl.ds(b * BLOCK, BLOCK)
        row = jnp.max(jnp.transpose(top[rows, :], (1, 0)), axis=0, keepdims=True)
        level[rows, :] = across(row)
        found.append(row)
    return found


def mask_of(ref, start=2 * SIDE):
    return jnp.sum(ref[start : start + 16, :].astype(F32)).astype(I32)


def here():
    return [lax.axis_index(a) for a in ("z", "x", "y", "core")]


def load_queries(q, q3):
    for b in range(8):
        q[pl.ds(b * BLOCK, BLOCK), :] = q3[b, 0:BLOCK, :]


def gather_kernel(queries, near, far, out):
    for b in range(8):
        out[b, 0:BLOCK, :] = queries[...]
        out[b, BLOCK : BLOCK + 16, :] = near[...]
        out[b, BLOCK + 16 : SENT, :] = far[...]


def rows_kernel(q3, af, bf, out):
    for b in range(8):
        out[b * 32 : b * 32 + 32, :] = q3[b, BLOCK:SENT, :]


def select_kernel(r0, r1, r2, r3, out):
    z = lax.axis_index("z")

    @pl.when(z < 4)
    def _():
        out[0:256, :] = r0[...]
        out[256:512, :] = r3[...]

    @pl.when(z >= 4)
    def _():
        out[0:256, :] = r1[...]
        out[256:512, :] = r2[...]


def first_kernel(
    table, live, q3, ok, ov, an, af, bn, bf, level, total, acc, q, scores, top
):
    load_queries(q, q3)
    top[...] = jnp.full(top.shape, NEG, F32)
    total[...] = jnp.zeros(total.shape, F32)
    acc[...] = jnp.zeros(acc.shape, F32)
    own = 0
    for k in range(PAGES):
        own = own + jnp.where(k < live[0], jnp.left_shift(1, table[0, k]), 0)
    stores = [
        (
            own,
            lambda p: [page_parts(ok, p, 0, KEYS), page_parts(ok, p, HALF, KEYS)],
            lambda p: [page_parts(ov, p, 0, KEYS), page_parts(ov, p, HALF, KEYS)],
        )
    ]
    for near, far in ((an, af), (bn, bf)):
        stores.append(
            (
                mask_of(near),
                lambda p, near=near, far=far: [page_parts(near, p), page_parts(far, p)],
                lambda p, near=near, far=far: [page_parts(near, p, SIDE), page_parts(far, p, SIDE)],
            )
        )
    for i, (mask, keys_at, _) in enumerate(stores):
        score_pages(q, scores, top, i * PAGES, mask, keys_at)
    settle(top, level)
    for i, (mask, _, values_at) in enumerate(stores):
        weigh_pages(scores, level, total, acc, i * PAGES, mask, values_at)


def second_kernel(
    q3, ckn, cvn, ckf, cvf, new, level_in, total_in, acc_in, out,
    q, scores, fresh, top, level, total, acc,
):
    z, x, y, core = here()
    load_queries(q, q3)
    top[...] = level_in[...]
    mask = mask_of(cvn, SIDE)
    score_pages(q, scores, top, 0, mask, lambda p: [page_parts(ckn, p), page_parts(ckf, p)])

    at = lax.broadcasted_iota(I32, (BLOCK, BLOCK), 0)
    place = lax.broadcasted_iota(I32, (BLOCK, BLOCK), 1) == (at % 64) * 2 + at // 64
    place = jnp.where(place, 1.0, 0.0).astype(BF16)
    apart = [
        jnp.dot(place, new[g * BLOCK : (g + 1) * BLOCK, :], preferred_element_type=F32).astype(BF16)
        for g in range(4)
    ]
    keys = jnp.concatenate([n[0:64, :] for n in apart], axis=0)
    values = jnp.concatenate([n[64:BLOCK, :] for n in apart], axis=0)
    slot = lax.broadcasted_iota(I32, (TILE, 256), 1)
    side = jnp.where(slot < 128, jnp.where(z < 4, 0, 3), jnp.where(z < 4, 2, 1))
    head = ((y + side) & 3) * 2 + (core ^ ((slot // 8) & 1))
    token = ((slot // 16) % 8 * 4 + ((x + z) & 3)) * 64 + head * 8 + slot % 8
    row = lax.broadcasted_iota(I32, (TILE, 256), 0)
    for t in range(QROWS // TILE):
        rows = pl.ds(t * TILE, TILE)
        s = lax.dot_general(q[rows, :], keys, (((1,), (1,)), ((), ())), preferred_element_type=F32)
        position = ((2 * t + row // BLOCK) * 4 + x) * 64 + (row % BLOCK) // 2
        s = jnp.where(token <= position, s, NEG)
        fresh[rows, :] = s
        top[rows, :] = jnp.maximum(top[rows, :], jnp.maximum(s[:, :HD], s[:, HD:]))
    peaks = settle(top, level)
    for t in range(QROWS // TILE):
        rows = pl.ds(t * TILE, TILE)
        factor = jnp.exp2((level_in[rows, :] - level[rows, :]) * SCALE)
        total[rows, :] = total_in[rows, :] * factor
        acc[rows, :] = acc_in[rows, :] * factor
    weigh_pages(
        scores, level, total, acc, 0, mask,
        lambda p: [page_parts(cvn, p), page_parts(cvf, p)],
    )
    weigh(lambda rows: fresh[rows, :], values, level, total, acc, 256)

    for j in range(8):
        rows = pl.ds(j * BLOCK, BLOCK)
        full = acc[rows, :]
        size = jnp.max(jnp.transpose(jnp.abs(full), (1, 0)), axis=0, keepdims=True)
        size = jnp.maximum(size, 1e-30)
        number = jnp.round(full * across(32767.0 / size)).astype(I32).astype(jnp.int16)
        weight = jnp.sum(jnp.transpose(total[rows, :], (1, 0)), axis=0, keepdims=True)
        stats = (
            split_fixed(peaks[j] * SCALE)
            + split_fixed(jnp.log2(weight))
            + split_fixed(jnp.log2(size))
        )
        stats = jnp.concatenate(stats + [jnp.zeros((10, BLOCK), I32)], axis=0)
        out[j] = jnp.concatenate([number, stats.astype(jnp.int16)], axis=0)


def merge_kernel(parts, out):
    stats = [parts[s, BLOCK:PAYLOAD, :].astype(I32) for s in range(8)]

    def rows(at):
        return jnp.concatenate(
            [join_fixed(s[at : at + 1, :], s[at + 1 : at + 2, :]) for s in stats], axis=0
        )

    peak, weight, size = rows(0), rows(2), rows(4)
    peak = peak - jnp.max(peak, axis=0, keepdims=True)
    whole = jnp.sum(jnp.exp2(peak + weight), axis=0, keepdims=True)
    factor = jnp.exp2(peak + size) / (whole * 32767.0)
    columns = jnp.transpose(factor, (1, 0))
    total = jnp.zeros((BLOCK, HD), F32)
    for s in range(8):
        total = total + parts[s, 0:BLOCK, :].astype(F32) * columns[:, s : s + 1]
    out[...] = total.astype(BF16)


def route_kernel(r0, r1, r2, r3, code, payload, o0, o1, o2, o3):
    z, x, y, core = here()
    target = lax.broadcasted_iota(I32, (4 * 256, 256), 0)
    lane = lax.broadcasted_iota(I32, (4 * 256, 256), 1)
    store = z * 4 + ((x + target // 256) & 3)
    want = jnp.where((target & 1) == (lane & 1), store * 128 + (target % 256) // 2, -1)
    total = jnp.zeros((4 * 256, HD), F32)
    for j, r in enumerate((r0, r1, r2, r3)):
        have = code[pl.ds((y + (0, 3, 1, 2)[j]) & 3, 1), :]
        chosen = jnp.where(want == have, 1.0, 0.0).astype(BF16)
        total = total + jnp.dot(chosen, r[...], preferred_element_type=F32)
    total = total.astype(BF16)
    for d, o in enumerate((o0, o1, o2, o3)):
        o[...] = total[d * 256 : (d + 1) * 256, :]


def place_kernel(n0, n1, n2, n3, out):
    total = n0[...].astype(F32) + n1[...].astype(F32)
    total = total + n2[...].astype(F32) + n3[...].astype(F32)
    out[...] = total.astype(BF16)


SMALL = pltpu.CompilerParams(vmem_limit_bytes=8 * 1024 * 1024)


def smem():
    return pl.BlockSpec(memory_space=pltpu.SMEM)


def vmem():
    return pl.BlockSpec(memory_space=pltpu.VMEM)


def cost(pages):
    return pl.CostEstimate(
        flops=4 * QROWS * KEYS * HD * pages,
        bytes_accessed=1 << 20,
        transcendentals=QROWS * KEYS * pages,
    )


def shards(
    queries, cache_keys, cache_values, page_table, page_count, new_kv, new_owner, new_offset
):
    z, x = lax.axis_index("z"), lax.axis_index("x")
    y, core = lax.axis_index("y"), lax.axis_index("core")

    bits = jnp.where(jnp.arange(PAGES) < page_count[0], 1 << page_table[0], 0)
    bits_row = jnp.pad(bits.astype(BF16)[None, :], ((0, 15), (0, HD - PAGES)))
    halves = [
        lax.dynamic_index_in_dim(a.reshape(PAGES, 2, HALF, HD), core, 1, keepdims=False).reshape(
            SIDE, HD
        )
        for a in (cache_keys, cache_values)
    ]
    halves = jnp.concatenate(halves + [bits_row], axis=0)
    an, bn = shifted(halves, "x", 1), shifted(halves, "x", -1)
    ckn, cvn = shifted(an[:SIDE], "x", 1), shifted(bn[SIDE:], "x", -1)
    af, bf, ckf, cvf = [swapped(a, "core", 1) for a in (an, bn, ckn, cvn)]

    near = new_kv.reshape(16, HD)
    far = swapped(near, "core", 1)
    sent = pl.pallas_call(
        gather_kernel,
        out_shape=jax.ShapeDtypeStruct((8, SENT, HD), BF16),
        in_specs=[vmem()] * 3,
        out_specs=vmem(),
        compiler_params=SMALL,
        name="gather",
    )(queries.reshape(BLOCK, HD), near, far)
    q3 = lax.all_to_all(sent, "z", 0, 0)
    rows = pl.pallas_call(
        rows_kernel,
        out_shape=jax.ShapeDtypeStruct((256, HD), BF16),
        in_specs=[vmem()] * 3,
        out_specs=vmem(),
        compiler_params=SMALL,
        name="rows",
    )(q3, af, bf)
    rows = [rows, shifted(rows, "y", 1), shifted(rows, "y", -1), shifted(rows, "y", 2)]

    state = jax.ShapeDtypeStruct((QROWS, HD), F32)
    params = pltpu.CompilerParams(vmem_limit_bytes=50 * 1024 * 1024)
    level, total, acc = pl.pallas_call(
        first_kernel,
        out_shape=(state,) * 3,
        in_specs=[smem()] * 2 + [vmem()] * 7,
        out_specs=(vmem(),) * 3,
        scratch_shapes=[
            pltpu.VMEM((QROWS, HD), BF16),
            pltpu.VMEM((3 * PAGES, QROWS, KEYS), F32),
            pltpu.VMEM((QROWS, HD), F32),
        ],
        compiler_params=params,
        cost_estimate=cost(8),
        name="first",
    )(page_table, page_count, q3, cache_keys, cache_values, an, af, bn, bf)
    new = pl.pallas_call(
        select_kernel,
        out_shape=jax.ShapeDtypeStruct((512, HD), BF16),
        in_specs=[vmem()] * 4,
        out_specs=vmem(),
        compiler_params=SMALL,
        name="select",
    )(*rows)
    new = lax.ppermute(
        new, ("z", "x"), [(p * 4 + (i + p) % 4, p * 4 + i) for p in range(8) for i in range(4)]
    )
    payload = pl.pallas_call(
        second_kernel,
        out_shape=jax.ShapeDtypeStruct((8, PAYLOAD, HD), jnp.int16),
        in_specs=[vmem()] * 9,
        out_specs=vmem(),
        scratch_shapes=[
            pltpu.VMEM((QROWS, HD), BF16),
            pltpu.VMEM((PAGES, QROWS, KEYS), F32),
            pltpu.VMEM((QROWS, 256), F32),
        ]
        + [pltpu.VMEM((QROWS, HD), F32)] * 4,
        compiler_params=params,
        cost_estimate=cost(1),
        name="second",
    )(q3, ckn, cvn, ckf, cvf, new, level, total, acc)

    code = (new_owner * 128 + new_offset).reshape(8, 4, 4, 2, 8)
    code = lax.dynamic_index_in_dim(code, x, 1, keepdims=False)
    code = jnp.where(core == 1, jnp.flip(code, 2), code)
    code = jnp.repeat(jnp.transpose(code, (1, 0, 2, 3)).reshape(4, 128), 2, axis=1)
    piece = jax.ShapeDtypeStruct((256, HD), BF16)
    t0, to_after, to_opposite, to_before = pl.pallas_call(
        route_kernel,
        out_shape=(piece,) * 4,
        in_specs=[vmem()] * 5 + [pl.BlockSpec(memory_space=pl.ANY)],
        out_specs=(vmem(),) * 4,
        compiler_params=SMALL,
        name="route",
    )(*rows, code, payload)
    t1 = shifted(to_after, "x", 1)
    t2 = shifted(to_before, "x", -1)
    t3 = shifted(to_opposite, "x", 2)
    parts = lax.all_to_all(payload, "z", 0, 0)
    attended = pl.pallas_call(
        merge_kernel,
        out_shape=jax.ShapeDtypeStruct((BLOCK, HD), BF16),
        in_specs=[vmem()],
        out_specs=vmem(),
        compiler_params=SMALL,
        name="merge",
    )(parts)
    appended = pl.pallas_call(
        place_kernel,
        out_shape=jax.ShapeDtypeStruct((256, HD), BF16),
        in_specs=[vmem()] * 4,
        out_specs=vmem(),
        compiler_params=SMALL,
        name="place",
    )(t0, t1, t2, t3)
    return attended.reshape(queries.shape), appended.reshape(BLOCK, 2, HD)


def solution(mesh):
    grid = Mesh(mesh.devices.reshape(8, 4, 4, 2), ("z", "x", "y", "core"))
    ctx, head = ("z", "x"), ("y", "core")
    in_specs = (
        P(ctx, head, None),
        P(ctx, None),
        P(ctx, None),
        P(ctx, None),
        P(ctx),
        P(ctx + head, None, None),
        P(),
        P(),
    )
    out_specs = (P(ctx, head, None), P(ctx, None, None))
    return jax.shard_map(shards, mesh=grid, in_specs=in_specs, out_specs=out_specs, check_vma=False)
```

```python
import functools
import math

import jax
import jax.numpy as jnp
from jax import lax
from jax.experimental import pallas as pl
from jax.experimental.pallas import tpu as pltpu
from jax.sharding import Mesh, PartitionSpec as P

F32 = jnp.float32
BF16 = jnp.bfloat16
I32 = jnp.int32
HD = 128
PAGES = 4
HALF = 256
KEYS = 2 * HALF
SIDE = PAGES * HALF
QROWS = 1024
TILE = 512
BLOCK = 128
NEG = -1e30
SCALE = 1.4426950408889634 / math.sqrt(HD)
FIXED = float(1 << 18)
PAYLOAD = 144
SENT = 160


def shifted(value, axis, steps):
    count = lax.axis_size(axis)
    return lax.ppermute(value, axis, [(i, (i + steps) % count) for i in range(count)])


def swapped(value, axis, bit):
    count = lax.axis_size(axis)
    return lax.ppermute(value, axis, [(i, i ^ bit) for i in range(count)])


def across(row):
    return jnp.transpose(jnp.broadcast_to(row, (BLOCK, BLOCK)), (1, 0))


def split_fixed(value):
    fixed = jnp.round(value * FIXED).astype(I32)
    return [fixed >> 16, (fixed & 0xFFFF) - 32768]


def join_fixed(high, low):
    return (high * 65536 + (low + 32768)).astype(F32) * (1.0 / FIXED)


def page_parts(ref, p, start=0, stride=HALF):
    return ref[pl.ds(pl.multiple_of(start + p * stride, HALF), HALF), :]


def take(q, keys, values, top, total, acc, visible=None):
    def scores(t):
        found = []
        for i, part in enumerate(keys):
            s = lax.dot_general(
                q[pl.ds(t * TILE, TILE), :],
                part,
                (((1,), (1,)), ((), ())),
                preferred_element_type=F32,
            )
            if visible is not None:
                s = jnp.where(visible(t), s, NEG)
            found += [s[:, :HD], s[:, HD:]]
        return found

    def add(t, parts):
        rows = pl.ds(t * TILE, TILE)
        best = jnp.max(functools.reduce(jnp.maximum, parts), axis=1, keepdims=True)
        old = top[rows, :]
        now = jnp.maximum(old, jnp.broadcast_to(best, (TILE, HD)))
        factor = jnp.exp2((old - now) * SCALE)
        parts = [jnp.exp2((s - now) * SCALE) for s in parts]
        total[rows, :] = total[rows, :] * factor + functools.reduce(jnp.add, parts)
        weight = jnp.concatenate([e.astype(BF16) for e in parts], axis=1)
        acc[rows, :] = acc[rows, :] * factor + jnp.dot(
            weight, values, preferred_element_type=F32
        )
        top[rows, :] = now

    following = scores(0)
    for t in range(QROWS // TILE):
        current = following
        if t + 1 < QROWS // TILE:
            following = scores(t + 1)
        add(t, current)


def take_pages(q, mask, keys_at, values_at, top, total, acc):
    def page(p, carry):
        @pl.when(((mask >> p) & 1) != 0)
        def _():
            take(q, keys_at(p), jnp.concatenate(values_at(p), axis=0), top, total, acc)

        return carry

    lax.fori_loop(0, PAGES, page, 0)


def mask_of(ref, start=2 * SIDE):
    return jnp.sum(ref[start : start + 16, :].astype(F32)).astype(I32)


def here():
    return [lax.axis_index(a) for a in ("z", "x", "y", "core")]


def load_queries(q, q3):
    for b in range(8):
        q[pl.ds(b * BLOCK, BLOCK), :] = q3[b, 0:BLOCK, :]


def gather_kernel(queries, near, far, out):
    for b in range(8):
        out[b, 0:BLOCK, :] = queries[...]
        out[b, BLOCK : BLOCK + 16, :] = near[...]
        out[b, BLOCK + 16 : SENT, :] = far[...]


def own_mask(table, live):
    mask = 0
    for k in range(PAGES):
        mask = mask + jnp.where(k < live[0], jnp.left_shift(1, table[0, k]), 0)
    return mask


def rows_kernel(q3, af, bf, out):
    for b in range(8):
        out[b * 32 : b * 32 + 32, :] = q3[b, BLOCK:SENT, :]


def select_kernel(r0, r1, r2, r3, out):
    z = lax.axis_index("z")

    @pl.when(z < 4)
    def _():
        out[0:256, :] = r0[...]
        out[256:512, :] = r3[...]

    @pl.when(z >= 4)
    def _():
        out[0:256, :] = r1[...]
        out[256:512, :] = r2[...]


def first_kernel(table, live, q3, ok, ov, an, af, bn, bf, top, total, acc, q):
    load_queries(q, q3)
    top[...] = jnp.full(top.shape, NEG, F32)
    total[...] = jnp.zeros(total.shape, F32)
    acc[...] = jnp.zeros(acc.shape, F32)
    take_pages(
        q,
        own_mask(table, live),
        lambda p: [page_parts(ok, p, 0, KEYS), page_parts(ok, p, HALF, KEYS)],
        lambda p: [page_parts(ov, p, 0, KEYS), page_parts(ov, p, HALF, KEYS)],
        top, total, acc,
    )
    for near, far in ((an, af), (bn, bf)):
        take_pages(
            q,
            mask_of(near),
            lambda p, near=near, far=far: [page_parts(near, p), page_parts(far, p)],
            lambda p, near=near, far=far: [page_parts(near, p, SIDE), page_parts(far, p, SIDE)],
            top, total, acc,
        )


def second_kernel(
    q3, ckn, cvn, ckf, cvf, new, top_in, total_in, acc_in, out, q, top, total, acc
):
    z, x, y, core = here()
    load_queries(q, q3)
    top[...] = top_in[...]
    total[...] = total_in[...]
    acc[...] = acc_in[...]
    take_pages(
        q,
        mask_of(cvn, SIDE),
        lambda p: [page_parts(ckn, p), page_parts(ckf, p)],
        lambda p: [page_parts(cvn, p), page_parts(cvf, p)],
        top, total, acc,
    )

    at = lax.broadcasted_iota(I32, (BLOCK, BLOCK), 0)
    place = lax.broadcasted_iota(I32, (BLOCK, BLOCK), 1) == (at % 64) * 2 + at // 64
    place = jnp.where(place, 1.0, 0.0).astype(BF16)
    apart = [
        jnp.dot(place, new[g * BLOCK : (g + 1) * BLOCK, :], preferred_element_type=F32).astype(BF16)
        for g in range(4)
    ]
    keys = jnp.concatenate([n[0:64, :] for n in apart], axis=0)
    values = jnp.concatenate([n[64:BLOCK, :] for n in apart], axis=0)
    slot = lax.broadcasted_iota(I32, (TILE, 256), 1)
    side = jnp.where(slot < 128, jnp.where(z < 4, 0, 3), jnp.where(z < 4, 2, 1))
    head = ((y + side) & 3) * 2 + (core ^ ((slot // 8) & 1))
    token = ((slot // 16) % 8 * 4 + ((x + z) & 3)) * 64 + head * 8 + slot % 8
    row = lax.broadcasted_iota(I32, (TILE, 256), 0)

    def visible(t):
        position = ((TILE // BLOCK * t + row // BLOCK) * 4 + x) * 64 + (row % BLOCK) // 2
        return token <= position

    take(q, [keys], values, top, total, acc, visible)

    for j in range(8):
        rows = pl.ds(j * BLOCK, BLOCK)
        full = acc[rows, :]
        size = jnp.max(jnp.transpose(jnp.abs(full), (1, 0)), axis=0, keepdims=True)
        size = jnp.maximum(size, 1.2e-34)
        number = jnp.round(full * across(32767.0 / size)).astype(I32).astype(jnp.int16)
        weight = jnp.sum(jnp.transpose(total[rows, :], (1, 0)), axis=0, keepdims=True)
        stats = (
            split_fixed(jnp.transpose(top[rows, :], (1, 0))[0:1, :] * SCALE)
            + split_fixed(jnp.log2(weight))
            + split_fixed(jnp.log2(size))
        )
        stats = jnp.concatenate(stats + [jnp.zeros((10, BLOCK), I32)], axis=0)
        out[j] = jnp.concatenate([number, stats.astype(jnp.int16)], axis=0)


def merge_kernel(parts, n0, n1, n2, n3, out, appended):
    stats = [parts[s, BLOCK:PAYLOAD, :].astype(I32) for s in range(8)]

    def rows(at):
        return jnp.concatenate(
            [join_fixed(s[at : at + 1, :], s[at + 1 : at + 2, :]) for s in stats], axis=0
        )

    peak, weight, size = rows(0), rows(2), rows(4)
    peak = peak - jnp.max(peak, axis=0, keepdims=True)
    whole = jnp.sum(jnp.exp2(peak + weight), axis=0, keepdims=True)
    factor = jnp.exp2(peak + size) / (whole * 32767.0)
    columns = jnp.transpose(factor, (1, 0))
    total = jnp.zeros((BLOCK, HD), F32)
    for s in range(8):
        total = total + parts[s, 0:BLOCK, :].astype(F32) * columns[:, s : s + 1]
    out[...] = total.astype(BF16)
    rows = n0[...].astype(F32) + n1[...].astype(F32)
    rows = rows + n2[...].astype(F32) + n3[...].astype(F32)
    appended[...] = rows.astype(BF16)


def route_kernel(r0, r1, r2, r3, code, payload, o0, o1, o2, o3):
    z, x, y, core = here()
    target = lax.broadcasted_iota(I32, (4 * 256, 256), 0)
    lane = lax.broadcasted_iota(I32, (4 * 256, 256), 1)
    store = z * 4 + ((x + target // 256) & 3)
    want = jnp.where((target & 1) == (lane & 1), store * 128 + (target % 256) // 2, -1)
    total = jnp.zeros((4 * 256, HD), F32)
    for j, r in enumerate((r0, r1, r2, r3)):
        have = code[pl.ds((y + (0, 3, 1, 2)[j]) & 3, 1), :]
        chosen = jnp.where(want == have, 1.0, 0.0).astype(BF16)
        total = total + jnp.dot(chosen, r[...], preferred_element_type=F32)
    total = total.astype(BF16)
    for d, o in enumerate((o0, o1, o2, o3)):
        o[...] = total[d * 256 : (d + 1) * 256, :]


SMALL = pltpu.CompilerParams(vmem_limit_bytes=8 * 1024 * 1024)


def smem():
    return pl.BlockSpec(memory_space=pltpu.SMEM)


def vmem():
    return pl.BlockSpec(memory_space=pltpu.VMEM)


def cost(pages):
    return pl.CostEstimate(
        flops=4 * QROWS * KEYS * HD * pages,
        bytes_accessed=1 << 20,
        transcendentals=QROWS * KEYS * pages,
    )


def shards(
    queries, cache_keys, cache_values, page_table, page_count, new_kv, new_owner, new_offset
):
    z, x = lax.axis_index("z"), lax.axis_index("x")
    y, core = lax.axis_index("y"), lax.axis_index("core")

    bits = jnp.where(jnp.arange(PAGES) < page_count[0], 1 << page_table[0], 0)
    bits_row = jnp.pad(bits.astype(BF16)[None, :], ((0, 15), (0, HD - PAGES)))
    halves = [
        lax.dynamic_index_in_dim(a.reshape(PAGES, 2, HALF, HD), core, 1, keepdims=False).reshape(
            SIDE, HD
        )
        for a in (cache_keys, cache_values)
    ]
    halves = jnp.concatenate(halves + [bits_row], axis=0)
    an, bn = shifted(halves, "x", 1), shifted(halves, "x", -1)
    ckn, cvn = shifted(an[:SIDE], "x", 1), shifted(bn[SIDE:], "x", -1)
    af, bf, ckf, cvf = [swapped(a, "core", 1) for a in (an, bn, ckn, cvn)]

    near = new_kv.reshape(16, HD)
    far = swapped(near, "core", 1)
    sent = pl.pallas_call(
        gather_kernel,
        out_shape=jax.ShapeDtypeStruct((8, SENT, HD), BF16),
        in_specs=[vmem()] * 3,
        out_specs=vmem(),
        compiler_params=SMALL,
        name="gather",
    )(queries.reshape(BLOCK, HD), near, far)
    q3 = lax.all_to_all(sent, "z", 0, 0)
    rows = pl.pallas_call(
        rows_kernel,
        out_shape=jax.ShapeDtypeStruct((256, HD), BF16),
        in_specs=[vmem()] * 3,
        out_specs=vmem(),
        compiler_params=SMALL,
        name="rows",
    )(q3, af, bf)
    opposite = shifted(rows, "y", 2)
    rows = [rows, shifted(rows, "y", 1), shifted(rows, "y", -1), opposite]

    state = jax.ShapeDtypeStruct((QROWS, HD), F32)
    params = pltpu.CompilerParams(vmem_limit_bytes=24 * 1024 * 1024)
    level, total, acc = pl.pallas_call(
        first_kernel,
        out_shape=(state,) * 3,
        in_specs=[smem()] * 2 + [vmem()] * 7,
        out_specs=(vmem(),) * 3,
        scratch_shapes=[pltpu.VMEM((QROWS, HD), BF16)],
        compiler_params=params,
        cost_estimate=cost(8),
        name="first",
    )(page_table, page_count, q3, cache_keys, cache_values, an, af, bn, bf)
    new = pl.pallas_call(
        select_kernel,
        out_shape=jax.ShapeDtypeStruct((512, HD), BF16),
        in_specs=[vmem()] * 4,
        out_specs=vmem(),
        compiler_params=SMALL,
        name="select",
    )(*rows)
    new = lax.ppermute(
        new, ("z", "x"), [(p * 4 + (i + p) % 4, p * 4 + i) for p in range(8) for i in range(4)]
    )
    payload = pl.pallas_call(
        second_kernel,
        out_shape=jax.ShapeDtypeStruct((8, PAYLOAD, HD), jnp.int16),
        in_specs=[vmem()] * 9,
        out_specs=vmem(),
        scratch_shapes=[pltpu.VMEM((QROWS, HD), BF16)] + [pltpu.VMEM((QROWS, HD), F32)] * 3,
        compiler_params=params,
        cost_estimate=cost(1),
        name="second",
    )(q3, ckn, cvn, ckf, cvf, new, level, total, acc)

    code = (new_owner * 128 + new_offset).reshape(8, 4, 4, 2, 8)
    code = lax.dynamic_index_in_dim(code, x, 1, keepdims=False)
    code = jnp.where(core == 1, jnp.flip(code, 2), code)
    code = jnp.repeat(jnp.transpose(code, (1, 0, 2, 3)).reshape(4, 128), 2, axis=1)
    piece = jax.ShapeDtypeStruct((256, HD), BF16)
    t0, to_after, to_opposite, to_before = pl.pallas_call(
        route_kernel,
        out_shape=(piece,) * 4,
        in_specs=[vmem()] * 5 + [pl.BlockSpec(memory_space=pl.ANY)],
        out_specs=(vmem(),) * 4,
        compiler_params=SMALL,
        name="route",
    )(*rows, code, payload)
    t3 = shifted(to_opposite, "x", 2)
    t1 = shifted(to_after, "x", 1)
    t2 = shifted(to_before, "x", -1)
    parts = lax.all_to_all(payload, "z", 0, 0)
    attended, appended = pl.pallas_call(
        merge_kernel,
        out_shape=(
            jax.ShapeDtypeStruct((BLOCK, HD), BF16),
            jax.ShapeDtypeStruct((256, HD), BF16),
        ),
        in_specs=[vmem()] * 5,
        out_specs=(vmem(),) * 2,
        compiler_params=SMALL,
        name="merge",
    )(parts, t0, t1, t2, t3)
    return attended.reshape(queries.shape), appended.reshape(BLOCK, 2, HD)


def solution(mesh):
    grid = Mesh(mesh.devices.reshape(8, 4, 4, 2), ("z", "x", "y", "core"))
    ctx, head = ("z", "x"), ("y", "core")
    in_specs = (
        P(ctx, head, None),
        P(ctx, None),
        P(ctx, None),
        P(ctx, None),
        P(ctx),
        P(ctx + head, None, None),
        P(),
        P(),
    )
    out_specs = (P(ctx, head, None), P(ctx, None, None))
    return jax.shard_map(shards, mesh=grid, in_specs=in_specs, out_specs=out_specs, check_vma=False)
```

```python
import functools
import math

import jax
import jax.numpy as jnp
from jax import lax
from jax.experimental import pallas as pl
from jax.experimental.pallas import tpu as pltpu
from jax.sharding import Mesh, PartitionSpec as P

F32 = jnp.float32
BF16 = jnp.bfloat16
I32 = jnp.int32
HD = 128
PAGES = 4
HALF = 256
KEYS = 2 * HALF
SIDE = PAGES * HALF
QROWS = 1024
TILE = 512
BLOCK = 128
NEG = -1e30
SCALE = 1.4426950408889634 / math.sqrt(HD)
FIXED = float(1 << 18)
PAYLOAD = 144
SENT = 160


def shifted(value, axis, steps):
    count = lax.axis_size(axis)
    return lax.ppermute(value, axis, [(i, (i + steps) % count) for i in range(count)])


def swapped(value, axis, bit):
    count = lax.axis_size(axis)
    return lax.ppermute(value, axis, [(i, i ^ bit) for i in range(count)])


def split_fixed(value):
    fixed = jnp.round(value * FIXED).astype(I32)
    return [fixed >> 16, (fixed & 0xFFFF) - 32768]


def join_fixed(high, low):
    return (high * 65536 + (low + 32768)).astype(F32) * (1.0 / FIXED)


def page_parts(ref, p, start=0, stride=HALF):
    return ref[pl.ds(pl.multiple_of(start + p * stride, HALF), HALF), :]


def take(q, keys, values, top, total, acc, visible=None):
    def scores(t):
        found = []
        for i, part in enumerate(keys):
            s = lax.dot_general(
                q[pl.ds(t * TILE, TILE), :],
                part,
                (((1,), (1,)), ((), ())),
                preferred_element_type=F32,
            )
            if visible is not None:
                s = jnp.where(visible(t), s, NEG)
            found += [s[:, :HD], s[:, HD:]]
        return found

    def add(t, parts):
        rows = pl.ds(t * TILE, TILE)
        best = jnp.max(functools.reduce(jnp.maximum, parts), axis=1, keepdims=True)
        old = top[rows, :]
        now = jnp.maximum(old, jnp.broadcast_to(best, (TILE, HD)))
        factor = jnp.exp2((old - now) * SCALE)
        parts = [jnp.exp2((s - now) * SCALE) for s in parts]
        total[rows, :] = total[rows, :] * factor + functools.reduce(jnp.add, parts)
        weight = jnp.concatenate([e.astype(BF16) for e in parts], axis=1)
        acc[rows, :] = acc[rows, :] * factor + jnp.dot(
            weight, values, preferred_element_type=F32
        )
        top[rows, :] = now

    following = scores(0)
    for t in range(QROWS // TILE):
        current = following
        if t + 1 < QROWS // TILE:
            following = scores(t + 1)
        add(t, current)


def take_pages(q, mask, keys_at, values_at, top, total, acc):
    def page(p, carry):
        @pl.when(((mask >> p) & 1) != 0)
        def _():
            take(q, keys_at(p), jnp.concatenate(values_at(p), axis=0), top, total, acc)

        return carry

    lax.fori_loop(0, PAGES, page, 0)


def mask_of(ref, start=2 * SIDE):
    return jnp.sum(ref[start : start + 16, :].astype(F32)).astype(I32)


def here():
    return [lax.axis_index(a) for a in ("z", "x", "y", "core")]


def load_queries(q, q3):
    for b in range(8):
        q[pl.ds(b * BLOCK, BLOCK), :] = q3[b, 0:BLOCK, :]


def gather_kernel(queries, near, far, out):
    for b in range(8):
        out[b, 0:BLOCK, :] = queries[...]
        out[b, BLOCK : BLOCK + 16, :] = near[...]
        out[b, BLOCK + 16 : SENT, :] = far[...]


def own_mask(table, live):
    mask = 0
    for k in range(PAGES):
        mask = mask + jnp.where(k < live[0], jnp.left_shift(1, table[0, k]), 0)
    return mask


def rows_kernel(q3, af, bf, out):
    for b in range(8):
        out[b * 32 : b * 32 + 32, :] = q3[b, BLOCK:SENT, :]


def select_kernel(r0, r1, r2, r3, out):
    z = lax.axis_index("z")

    @pl.when(z < 4)
    def _():
        out[0:256, :] = r0[...]
        out[256:512, :] = r3[...]

    @pl.when(z >= 4)
    def _():
        out[0:256, :] = r1[...]
        out[256:512, :] = r2[...]


def first_kernel(table, live, q3, ok, ov, an, af, bn, bf, top, total, acc, q):
    load_queries(q, q3)
    top[...] = jnp.full(top.shape, NEG, F32)
    total[...] = jnp.zeros(total.shape, F32)
    acc[...] = jnp.zeros(acc.shape, F32)
    take_pages(
        q,
        own_mask(table, live),
        lambda p: [page_parts(ok, p, 0, KEYS), page_parts(ok, p, HALF, KEYS)],
        lambda p: [page_parts(ov, p, 0, KEYS), page_parts(ov, p, HALF, KEYS)],
        top, total, acc,
    )
    for near, far in ((an, af), (bn, bf)):
        take_pages(
            q,
            mask_of(near),
            lambda p, near=near, far=far: [page_parts(near, p), page_parts(far, p)],
            lambda p, near=near, far=far: [page_parts(near, p, SIDE), page_parts(far, p, SIDE)],
            top, total, acc,
        )


def second_kernel(
    q3, ckn, cvn, ckf, cvf, new, top_in, total_in, acc_in, out, q, top, total, acc
):
    z, x, y, core = here()
    load_queries(q, q3)
    top[...] = top_in[...]
    total[...] = total_in[...]
    acc[...] = acc_in[...]
    take_pages(
        q,
        mask_of(cvn, SIDE),
        lambda p: [page_parts(ckn, p), page_parts(ckf, p)],
        lambda p: [page_parts(cvn, p), page_parts(cvf, p)],
        top, total, acc,
    )

    at = lax.broadcasted_iota(I32, (BLOCK, BLOCK), 0)
    place = lax.broadcasted_iota(I32, (BLOCK, BLOCK), 1) == (at % 64) * 2 + at // 64
    place = jnp.where(place, 1.0, 0.0).astype(BF16)
    apart = [
        jnp.dot(place, new[g * BLOCK : (g + 1) * BLOCK, :], preferred_element_type=F32).astype(BF16)
        for g in range(4)
    ]
    keys = jnp.concatenate([n[0:64, :] for n in apart], axis=0)
    values = jnp.concatenate([n[64:BLOCK, :] for n in apart], axis=0)
    slot = lax.broadcasted_iota(I32, (TILE, 256), 1)
    side = jnp.where(slot < 128, jnp.where(z < 4, 0, 3), jnp.where(z < 4, 2, 1))
    head = ((y + side) & 3) * 2 + (core ^ ((slot // 8) & 1))
    token = ((slot // 16) % 8 * 4 + ((x + z) & 3)) * 64 + head * 8 + slot % 8
    row = lax.broadcasted_iota(I32, (TILE, 256), 0)

    def visible(t):
        position = ((TILE // BLOCK * t + row // BLOCK) * 4 + x) * 64 + (row % BLOCK) // 2
        return token <= position

    take(q, [keys], values, top, total, acc, visible)

    lane = lax.broadcasted_iota(I32, (BLOCK, BLOCK), 1)
    for j in range(8):
        rows = pl.ds(j * BLOCK, BLOCK)
        full = acc[rows, :]
        size = jnp.maximum(jnp.max(jnp.abs(full), axis=1, keepdims=True), 1.2e-34)
        number = jnp.round(full * (32767.0 / size)).astype(I32).astype(jnp.int16)
        weight = jnp.sum(total[rows, :], axis=1, keepdims=True)
        turned = jnp.where(lane == 0, top[rows, :], jnp.where(lane == 1, weight, size))
        turned = jnp.transpose(turned, (1, 0))
        stats = (
            split_fixed(turned[0:1, :] * SCALE)
            + split_fixed(jnp.log2(turned[1:2, :]))
            + split_fixed(jnp.log2(turned[2:3, :]))
        )
        stats = jnp.concatenate(stats + [jnp.zeros((10, BLOCK), I32)], axis=0)
        out[j] = jnp.concatenate([number, stats.astype(jnp.int16)], axis=0)


def merge_kernel(parts, n0, n1, n2, n3, out, appended):
    stats = [parts[s, BLOCK:PAYLOAD, :].astype(I32) for s in range(8)]

    def rows(at):
        return jnp.concatenate(
            [join_fixed(s[at : at + 1, :], s[at + 1 : at + 2, :]) for s in stats], axis=0
        )

    peak, weight, size = rows(0), rows(2), rows(4)
    peak = peak - jnp.max(peak, axis=0, keepdims=True)
    whole = jnp.sum(jnp.exp2(peak + weight), axis=0, keepdims=True)
    factor = jnp.exp2(peak + size) / (whole * 32767.0)
    columns = jnp.transpose(factor, (1, 0))
    total = jnp.zeros((BLOCK, HD), F32)
    for s in range(8):
        total = total + parts[s, 0:BLOCK, :].astype(F32) * columns[:, s : s + 1]
    out[...] = total.astype(BF16)
    rows = n0[...].astype(F32) + n1[...].astype(F32)
    rows = rows + n2[...].astype(F32) + n3[...].astype(F32)
    appended[...] = rows.astype(BF16)


def route_kernel(r0, r1, r2, r3, code, payload, o0, o1, o2, o3):
    z, x, y, core = here()
    target = lax.broadcasted_iota(I32, (4 * 256, 256), 0)
    lane = lax.broadcasted_iota(I32, (4 * 256, 256), 1)
    store = z * 4 + ((x + target // 256) & 3)
    want = jnp.where((target & 1) == (lane & 1), store * 128 + (target % 256) // 2, -1)
    total = jnp.zeros((4 * 256, HD), F32)
    for j, r in enumerate((r0, r1, r2, r3)):
        have = code[pl.ds((y + (0, 3, 1, 2)[j]) & 3, 1), :]
        chosen = jnp.where(want == have, 1.0, 0.0).astype(BF16)
        total = total + jnp.dot(chosen, r[...], preferred_element_type=F32)
    total = total.astype(BF16)
    for d, o in enumerate((o0, o1, o2, o3)):
        o[...] = total[d * 256 : (d + 1) * 256, :]


SMALL = pltpu.CompilerParams(vmem_limit_bytes=8 * 1024 * 1024)


def smem():
    return pl.BlockSpec(memory_space=pltpu.SMEM)


def vmem():
    return pl.BlockSpec(memory_space=pltpu.VMEM)


def cost(pages):
    return pl.CostEstimate(
        flops=4 * QROWS * KEYS * HD * pages,
        bytes_accessed=1 << 20,
        transcendentals=QROWS * KEYS * pages,
    )


def shards(
    queries, cache_keys, cache_values, page_table, page_count, new_kv, new_owner, new_offset
):
    z, x = lax.axis_index("z"), lax.axis_index("x")
    y, core = lax.axis_index("y"), lax.axis_index("core")

    bits = jnp.where(jnp.arange(PAGES) < page_count[0], 1 << page_table[0], 0)
    bits_row = jnp.pad(bits.astype(BF16)[None, :], ((0, 15), (0, HD - PAGES)))
    halves = [
        lax.dynamic_index_in_dim(a.reshape(PAGES, 2, HALF, HD), core, 1, keepdims=False).reshape(
            SIDE, HD
        )
        for a in (cache_keys, cache_values)
    ]
    halves = jnp.concatenate(halves + [bits_row], axis=0)
    an, bn = shifted(halves, "x", 1), shifted(halves, "x", -1)
    ckn, cvn = shifted(an[:SIDE], "x", 1), shifted(bn[SIDE:], "x", -1)
    af, bf, ckf, cvf = [swapped(a, "core", 1) for a in (an, bn, ckn, cvn)]

    near = new_kv.reshape(16, HD)
    far = swapped(near, "core", 1)
    sent = pl.pallas_call(
        gather_kernel,
        out_shape=jax.ShapeDtypeStruct((8, SENT, HD), BF16),
        in_specs=[vmem()] * 3,
        out_specs=vmem(),
        compiler_params=SMALL,
        name="gather",
    )(queries.reshape(BLOCK, HD), near, far)
    q3 = lax.all_to_all(sent, "z", 0, 0)
    rows = pl.pallas_call(
        rows_kernel,
        out_shape=jax.ShapeDtypeStruct((256, HD), BF16),
        in_specs=[vmem()] * 3,
        out_specs=vmem(),
        compiler_params=SMALL,
        name="rows",
    )(q3, af, bf)
    opposite = shifted(rows, "y", 2)
    rows = [rows, shifted(rows, "y", 1), shifted(rows, "y", -1), opposite]

    state = jax.ShapeDtypeStruct((QROWS, HD), F32)
    params = pltpu.CompilerParams(vmem_limit_bytes=24 * 1024 * 1024)
    level, total, acc = pl.pallas_call(
        first_kernel,
        out_shape=(state,) * 3,
        in_specs=[smem()] * 2 + [vmem()] * 7,
        out_specs=(vmem(),) * 3,
        scratch_shapes=[pltpu.VMEM((QROWS, HD), BF16)],
        compiler_params=params,
        cost_estimate=cost(8),
        name="first",
    )(page_table, page_count, q3, cache_keys, cache_values, an, af, bn, bf)
    new = pl.pallas_call(
        select_kernel,
        out_shape=jax.ShapeDtypeStruct((512, HD), BF16),
        in_specs=[vmem()] * 4,
        out_specs=vmem(),
        compiler_params=SMALL,
        name="select",
    )(*rows)
    new = lax.ppermute(
        new, ("z", "x"), [(p * 4 + (i + p) % 4, p * 4 + i) for p in range(8) for i in range(4)]
    )
    payload = pl.pallas_call(
        second_kernel,
        out_shape=jax.ShapeDtypeStruct((8, PAYLOAD, HD), jnp.int16),
        in_specs=[vmem()] * 9,
        out_specs=vmem(),
        scratch_shapes=[pltpu.VMEM((QROWS, HD), BF16)] + [pltpu.VMEM((QROWS, HD), F32)] * 3,
        compiler_params=params,
        cost_estimate=cost(1),
        name="second",
    )(q3, ckn, cvn, ckf, cvf, new, level, total, acc)

    code = (new_owner * 128 + new_offset).reshape(8, 4, 4, 2, 8)
    code = lax.dynamic_index_in_dim(code, x, 1, keepdims=False)
    code = jnp.where(core == 1, jnp.flip(code, 2), code)
    code = jnp.repeat(jnp.transpose(code, (1, 0, 2, 3)).reshape(4, 128), 2, axis=1)
    piece = jax.ShapeDtypeStruct((256, HD), BF16)
    t0, to_after, to_opposite, to_before = pl.pallas_call(
        route_kernel,
        out_shape=(piece,) * 4,
        in_specs=[vmem()] * 5 + [pl.BlockSpec(memory_space=pl.ANY)],
        out_specs=(vmem(),) * 4,
        compiler_params=SMALL,
        name="route",
    )(*rows, code, payload)
    t3 = shifted(to_opposite, "x", 2)
    t1 = shifted(to_after, "x", 1)
    t2 = shifted(to_before, "x", -1)
    parts = lax.all_to_all(payload, "z", 0, 0)
    attended, appended = pl.pallas_call(
        merge_kernel,
        out_shape=(
            jax.ShapeDtypeStruct((BLOCK, HD), BF16),
            jax.ShapeDtypeStruct((256, HD), BF16),
        ),
        in_specs=[vmem()] * 5,
        out_specs=(vmem(),) * 2,
        compiler_params=SMALL,
        name="merge",
    )(parts, t3, t2, t1, t0)
    return attended.reshape(queries.shape), appended.reshape(BLOCK, 2, HD)


def solution(mesh):
    grid = Mesh(mesh.devices.reshape(8, 4, 4, 2), ("z", "x", "y", "core"))
    ctx, head = ("z", "x"), ("y", "core")
    in_specs = (
        P(ctx, head, None),
        P(ctx, None),
        P(ctx, None),
        P(ctx, None),
        P(ctx),
        P(ctx + head, None, None),
        P(),
        P(),
    )
    out_specs = (P(ctx, head, None), P(ctx, None, None))
    return jax.shard_map(shards, mesh=grid, in_specs=in_specs, out_specs=out_specs, check_vma=False)
```

```python
import functools
import math

import jax
import jax.numpy as jnp
from jax import lax
from jax.experimental import pallas as pl
from jax.experimental.pallas import tpu as pltpu
from jax.sharding import Mesh, PartitionSpec as P

F32 = jnp.float32
BF16 = jnp.bfloat16
I32 = jnp.int32
HD = 128
PAGES = 4
HALF = 256
KEYS = 2 * HALF
SIDE = PAGES * HALF
QROWS = 1024
TILE = 512
BLOCK = 128
NEG = -1e30
SCALE = 1.4426950408889634 / math.sqrt(HD)
FIXED = float(1 << 18)
PAYLOAD = 144
SENT = 160


def shifted(value, axis, steps):
    count = lax.axis_size(axis)
    return lax.ppermute(value, axis, [(i, (i + steps) % count) for i in range(count)])


def swapped(value, axis, bit):
    count = lax.axis_size(axis)
    return lax.ppermute(value, axis, [(i, i ^ bit) for i in range(count)])


def across(row):
    return jnp.transpose(jnp.broadcast_to(row, (BLOCK, BLOCK)), (1, 0))


def split_fixed(value):
    fixed = jnp.round(value * FIXED).astype(I32)
    return [fixed >> 16, (fixed & 0xFFFF) - 32768]


def join_fixed(high, low):
    return (high * 65536 + (low + 32768)).astype(F32) * (1.0 / FIXED)


def page_parts(ref, p, start=0, stride=HALF):
    return ref[pl.ds(pl.multiple_of(start + p * stride, HALF), HALF), :]


def take(q, keys, values, top, total, acc, visible=None):
    def scores(t):
        found = []
        for i, part in enumerate(keys):
            s = lax.dot_general(
                q[pl.ds(t * TILE, TILE), :],
                part,
                (((1,), (1,)), ((), ())),
                preferred_element_type=F32,
            )
            if visible is not None:
                s = jnp.where(visible(t), s, NEG)
            found += [s[:, :HD], s[:, HD:]]
        return found

    def add(t, parts):
        rows = pl.ds(t * TILE, TILE)
        best = jnp.max(functools.reduce(jnp.maximum, parts), axis=1, keepdims=True)
        old = top[rows, :]
        now = jnp.maximum(old, jnp.broadcast_to(best, (TILE, HD)))
        factor = jnp.exp2((old - now) * SCALE)
        parts = [jnp.exp2((s - now) * SCALE) for s in parts]
        total[rows, :] = total[rows, :] * factor + functools.reduce(jnp.add, parts)
        weight = jnp.concatenate([e.astype(BF16) for e in parts], axis=1)
        acc[rows, :] = acc[rows, :] * factor + jnp.dot(
            weight, values, preferred_element_type=F32
        )
        top[rows, :] = now

    following = scores(0)
    for t in range(QROWS // TILE):
        current = following
        if t + 1 < QROWS // TILE:
            following = scores(t + 1)
        add(t, current)


def take_pages(q, mask, keys_at, values_at, top, total, acc):
    def page(p, carry):
        @pl.when(((mask >> p) & 1) != 0)
        def _():
            take(q, keys_at(p), jnp.concatenate(values_at(p), axis=0), top, total, acc)

        return carry

    lax.fori_loop(0, PAGES, page, 0)


def mask_of(ref, start=2 * SIDE):
    return jnp.sum(ref[start : start + 16, :].astype(F32)).astype(I32)


def here():
    return [lax.axis_index(a) for a in ("z", "x", "y", "core")]


def load_queries(q, q3):
    for b in range(8):
        q[pl.ds(b * BLOCK, BLOCK), :] = q3[b, 0:BLOCK, :]


def gather_kernel(queries, near, far, out):
    for b in range(8):
        out[b, 0:BLOCK, :] = queries[...]
        out[b, BLOCK : BLOCK + 16, :] = near[...]
        out[b, BLOCK + 16 : SENT, :] = far[...]


def own_mask(table, live):
    mask = 0
    for k in range(PAGES):
        mask = mask + jnp.where(k < live[0], jnp.left_shift(1, table[0, k]), 0)
    return mask


def rows_kernel(q3, af, bf, ok, ov, out):
    for b in range(8):
        out[b * 32 : b * 32 + 32, :] = q3[b, BLOCK:SENT, :]


def select_kernel(r0, r1, r2, r3, out):
    z = lax.axis_index("z")

    @pl.when(z < 4)
    def _():
        out[0:256, :] = r0[...]
        out[256:512, :] = r3[...]

    @pl.when(z >= 4)
    def _():
        out[0:256, :] = r1[...]
        out[256:512, :] = r2[...]


def first_kernel(table, live, q3, ok, ov, an, af, bn, bf, top, total, acc, q):
    load_queries(q, q3)
    top[...] = jnp.full(top.shape, NEG, F32)
    total[...] = jnp.zeros(total.shape, F32)
    acc[...] = jnp.zeros(acc.shape, F32)
    take_pages(
        q,
        own_mask(table, live),
        lambda p: [page_parts(ok, p, 0, KEYS), page_parts(ok, p, HALF, KEYS)],
        lambda p: [page_parts(ov, p, 0, KEYS), page_parts(ov, p, HALF, KEYS)],
        top, total, acc,
    )
    for near, far in ((an, af), (bn, bf)):
        take_pages(
            q,
            mask_of(near),
            lambda p, near=near, far=far: [page_parts(near, p), page_parts(far, p)],
            lambda p, near=near, far=far: [page_parts(near, p, SIDE), page_parts(far, p, SIDE)],
            top, total, acc,
        )


def second_kernel(
    q3, ckn, cvn, ckf, cvf, new, top_in, total_in, acc_in, out, q, top, total, acc
):
    z, x, y, core = here()
    load_queries(q, q3)
    top[...] = top_in[...]
    total[...] = total_in[...]
    acc[...] = acc_in[...]
    take_pages(
        q,
        mask_of(cvn, SIDE),
        lambda p: [page_parts(ckn, p), page_parts(ckf, p)],
        lambda p: [page_parts(cvn, p), page_parts(cvf, p)],
        top, total, acc,
    )

    at = lax.broadcasted_iota(I32, (BLOCK, BLOCK), 0)
    place = lax.broadcasted_iota(I32, (BLOCK, BLOCK), 1) == (at % 64) * 2 + at // 64
    place = jnp.where(place, 1.0, 0.0).astype(BF16)
    apart = [
        jnp.dot(place, new[g * BLOCK : (g + 1) * BLOCK, :], preferred_element_type=F32).astype(BF16)
        for g in range(4)
    ]
    keys = jnp.concatenate([n[0:64, :] for n in apart], axis=0)
    values = jnp.concatenate([n[64:BLOCK, :] for n in apart], axis=0)
    slot = lax.broadcasted_iota(I32, (TILE, 256), 1)
    side = jnp.where(slot < 128, jnp.where(z < 4, 0, 3), jnp.where(z < 4, 2, 1))
    head = ((y + side) & 3) * 2 + (core ^ ((slot // 8) & 1))
    token = ((slot // 16) % 8 * 4 + ((x + z) & 3)) * 64 + head * 8 + slot % 8
    row = lax.broadcasted_iota(I32, (TILE, 256), 0)

    def visible(t):
        position = ((TILE // BLOCK * t + row // BLOCK) * 4 + x) * 64 + (row % BLOCK) // 2
        return token <= position

    take(q, [keys], values, top, total, acc, visible)

    for j in range(8):
        rows = pl.ds(j * BLOCK, BLOCK)
        full = acc[rows, :]
        size = jnp.max(jnp.transpose(jnp.abs(full), (1, 0)), axis=0, keepdims=True)
        size = jnp.maximum(size, 1.2e-34)
        number = jnp.round(full * across(32767.0 / size)).astype(I32).astype(jnp.int16)
        weight = jnp.sum(jnp.transpose(total[rows, :], (1, 0)), axis=0, keepdims=True)
        stats = (
            split_fixed(jnp.transpose(top[rows, :], (1, 0))[0:1, :] * SCALE)
            + split_fixed(jnp.log2(weight))
            + split_fixed(jnp.log2(size))
        )
        stats = jnp.concatenate(stats + [jnp.zeros((10, BLOCK), I32)], axis=0)
        out[j] = jnp.concatenate([number, stats.astype(jnp.int16)], axis=0)


def merge_kernel(parts, n0, n1, n2, n3, out, appended):
    stats = [parts[s, BLOCK:PAYLOAD, :].astype(I32) for s in range(8)]

    def rows(at):
        return jnp.concatenate(
            [join_fixed(s[at : at + 1, :], s[at + 1 : at + 2, :]) for s in stats], axis=0
        )

    peak, weight, size = rows(0), rows(2), rows(4)
    peak = peak - jnp.max(peak, axis=0, keepdims=True)
    whole = jnp.sum(jnp.exp2(peak + weight), axis=0, keepdims=True)
    factor = jnp.exp2(peak + size) / (whole * 32767.0)
    columns = jnp.transpose(factor, (1, 0))
    total = jnp.zeros((BLOCK, HD), F32)
    for s in range(8):
        total = total + parts[s, 0:BLOCK, :].astype(F32) * columns[:, s : s + 1]
    out[...] = total.astype(BF16)
    rows = n0[...].astype(F32) + n1[...].astype(F32)
    rows = rows + n2[...].astype(F32) + n3[...].astype(F32)
    appended[...] = rows.astype(BF16)


def route_kernel(r0, r1, r2, r3, code, payload, o0, o1, o2, o3):
    z, x, y, core = here()
    target = lax.broadcasted_iota(I32, (4 * 256, 256), 0)
    lane = lax.broadcasted_iota(I32, (4 * 256, 256), 1)
    store = z * 4 + ((x + target // 256) & 3)
    want = jnp.where((target & 1) == (lane & 1), store * 128 + (target % 256) // 2, -1)
    total = jnp.zeros((4 * 256, HD), F32)
    for j, r in enumerate((r0, r1, r2, r3)):
        have = code[pl.ds((y + (0, 3, 1, 2)[j]) & 3, 1), :]
        chosen = jnp.where(want == have, 1.0, 0.0).astype(BF16)
        total = total + jnp.dot(chosen, r[...], preferred_element_type=F32)
    total = total.astype(BF16)
    for d, o in enumerate((o0, o1, o2, o3)):
        o[...] = total[d * 256 : (d + 1) * 256, :]


SMALL = pltpu.CompilerParams(vmem_limit_bytes=8 * 1024 * 1024)


def smem():
    return pl.BlockSpec(memory_space=pltpu.SMEM)


def vmem():
    return pl.BlockSpec(memory_space=pltpu.VMEM)


def cost(pages):
    return pl.CostEstimate(
        flops=4 * QROWS * KEYS * HD * pages,
        bytes_accessed=1 << 20,
        transcendentals=QROWS * KEYS * pages,
    )


def shards(
    queries, cache_keys, cache_values, page_table, page_count, new_kv, new_owner, new_offset
):
    z, x = lax.axis_index("z"), lax.axis_index("x")
    y, core = lax.axis_index("y"), lax.axis_index("core")

    bits = jnp.where(jnp.arange(PAGES) < page_count[0], 1 << page_table[0], 0)
    bits_row = jnp.pad(bits.astype(BF16)[None, :], ((0, 15), (0, HD - PAGES)))
    halves = [
        lax.dynamic_index_in_dim(a.reshape(PAGES, 2, HALF, HD), core, 1, keepdims=False).reshape(
            SIDE, HD
        )
        for a in (cache_keys, cache_values)
    ]
    halves = jnp.concatenate(halves + [bits_row], axis=0)
    an, bn = shifted(halves, "x", 1), shifted(halves, "x", -1)
    ckn, cvn = shifted(an[:SIDE], "x", 1), shifted(bn[SIDE:], "x", -1)
    af, bf, ckf, cvf = [swapped(a, "core", 1) for a in (an, bn, ckn, cvn)]

    near = new_kv.reshape(16, HD)
    far = swapped(near, "core", 1)
    sent = pl.pallas_call(
        gather_kernel,
        out_shape=jax.ShapeDtypeStruct((8, SENT, HD), BF16),
        in_specs=[vmem()] * 3,
        out_specs=vmem(),
        compiler_params=SMALL,
        name="gather",
    )(queries.reshape(BLOCK, HD), near, far)
    q3 = lax.all_to_all(sent, "z", 0, 0)
    rows = pl.pallas_call(
        rows_kernel,
        out_shape=jax.ShapeDtypeStruct((256, HD), BF16),
        in_specs=[vmem()] * 5,
        out_specs=vmem(),
        compiler_params=SMALL,
        name="rows",
    )(q3, af, bf, cache_keys, cache_values)
    opposite = shifted(rows, "y", 2)
    rows = [rows, shifted(rows, "y", 1), shifted(rows, "y", -1), opposite]

    state = jax.ShapeDtypeStruct((QROWS, HD), F32)
    params = pltpu.CompilerParams(vmem_limit_bytes=24 * 1024 * 1024)
    level, total, acc = pl.pallas_call(
        first_kernel,
        out_shape=(state,) * 3,
        in_specs=[smem()] * 2 + [vmem()] * 7,
        out_specs=(vmem(),) * 3,
        scratch_shapes=[pltpu.VMEM((QROWS, HD), BF16)],
        compiler_params=params,
        cost_estimate=cost(8),
        name="first",
    )(page_table, page_count, q3, cache_keys, cache_values, an, af, bn, bf)
    new = pl.pallas_call(
        select_kernel,
        out_shape=jax.ShapeDtypeStruct((512, HD), BF16),
        in_specs=[vmem()] * 4,
        out_specs=vmem(),
        compiler_params=SMALL,
        name="select",
    )(*rows)
    new = lax.ppermute(
        new, ("z", "x"), [(p * 4 + (i + p) % 4, p * 4 + i) for p in range(8) for i in range(4)]
    )
    payload = pl.pallas_call(
        second_kernel,
        out_shape=jax.ShapeDtypeStruct((8, PAYLOAD, HD), jnp.int16),
        in_specs=[vmem()] * 9,
        out_specs=vmem(),
        scratch_shapes=[pltpu.VMEM((QROWS, HD), BF16)] + [pltpu.VMEM((QROWS, HD), F32)] * 3,
        compiler_params=params,
        cost_estimate=cost(1),
        name="second",
    )(q3, ckn, cvn, ckf, cvf, new, level, total, acc)

    code = (new_owner * 128 + new_offset).reshape(8, 4, 4, 2, 8)
    code = lax.dynamic_index_in_dim(code, x, 1, keepdims=False)
    code = jnp.where(core == 1, jnp.flip(code, 2), code)
    code = jnp.repeat(jnp.transpose(code, (1, 0, 2, 3)).reshape(4, 128), 2, axis=1)
    piece = jax.ShapeDtypeStruct((256, HD), BF16)
    t0, to_after, to_opposite, to_before = pl.pallas_call(
        route_kernel,
        out_shape=(piece,) * 4,
        in_specs=[vmem()] * 5 + [pl.BlockSpec(memory_space=pl.ANY)],
        out_specs=(vmem(),) * 4,
        compiler_params=SMALL,
        name="route",
    )(*rows, code, payload)
    t3 = shifted(to_opposite, "x", 2)
    t1 = shifted(to_after, "x", 1)
    t2 = shifted(to_before, "x", -1)
    parts = lax.all_to_all(payload, "z", 0, 0)
    attended, appended = pl.pallas_call(
        merge_kernel,
        out_shape=(
            jax.ShapeDtypeStruct((BLOCK, HD), BF16),
            jax.ShapeDtypeStruct((256, HD), BF16),
        ),
        in_specs=[vmem()] * 5,
        out_specs=(vmem(),) * 2,
        compiler_params=SMALL,
        name="merge",
    )(parts, t0, t1, t2, t3)
    return attended.reshape(queries.shape), appended.reshape(BLOCK, 2, HD)


def solution(mesh):
    grid = Mesh(mesh.devices.reshape(8, 4, 4, 2), ("z", "x", "y", "core"))
    ctx, head = ("z", "x"), ("y", "core")
    in_specs = (
        P(ctx, head, None),
        P(ctx, None),
        P(ctx, None),
        P(ctx, None),
        P(ctx),
        P(ctx + head, None, None),
        P(),
        P(),
    )
    out_specs = (P(ctx, head, None), P(ctx, None, None))
    return jax.shard_map(shards, mesh=grid, in_specs=in_specs, out_specs=out_specs, check_vma=False)
```
